32 devices in a mesh: grp: 2 (over x), seq: 4 (over y, core), pair: 4 (over z).
Axes of the slice: x: 2, y: 2, z: 4, core: 2. Of those that a mesh axis runs over, the one named last changes fastest.
Arguments:
- seq_input: bfloat16 [8, 256, 1536], P(('grp', 'pair'), 'seq'), parts along dimension 0, may hold values from -6 to 6
- skip_input: bfloat16 [8, 512, 1536], P(('grp', 'pair'), 'seq'), parts along dimension 0, may hold values from -6 to 6
- norm_gain: float32 [1536], replicated, may hold values from 0.5 to 1.5
- query_weight: bfloat16 [1536, 512], replicated, may hold values from -2 to 2
- key_weight: bfloat16 [1536, 512], replicated, may hold values from -2 to 2
- value_weight: bfloat16 [1536, 1536], replicated, may hold values from -0.15625 to 0.15625
- conv_weight: float32 [3, 1536], replicated, may hold values from -3 to 3
- head_weight: bfloat16 [1536, 4096], P(None, 'pair'), may hold values from -0.15625 to 0.15625
- head_bias: float32 [4096], P('pair'), may hold values from -4 to 4
- exon_start: int32 [4, 64], P('grp'), parts along dimension 0, may hold values from 0 to 496
- exon_length: int32 [4, 64], P('grp'), parts along dimension 0, may hold values from 1 to 16
- exon_gene: int32 [4, 64], P('grp'), parts along dimension 0, may hold values from 0 to 7, as said below
- gene_order: int32 [4, 8], P('grp'), parts along dimension 0, may hold values from 0 to 7, each once within a row
Outputs:
- scores: float32 [4, 8, 4096], P('grp', 'seq', 'pair'), parts along dimension 0
The draws below stay inside these ranges and needn't reach their ends.
There are 2 independent parts, one for each index of `grp`. The reference program is written for one: setup_inputs(seed, part) draws one part's arguments, and reference() takes and returns one part's arrays. A program takes and returns all parts, laid end to end along the dimension named above; an argument that names none is the same for every part. Nothing has to cross between parts.
Inputs may be any that keep to these rules, and one draw needn't show every extreme that they name: `exon_gene`: every gene has at least one exon record. `gene_order`: each row names every gene once; the device at index s along seq owns positions s * 2 to (s + 1) * 2 - 1.
All inputs are finite; a program needn't handle non-finite values.
Results may differ from the reference program's by a relative error of at most 0.012.
Values may be sent and summed in bfloat16 or wider, within the bound.
A program may use at most 128 MiB of HBM per device.

```python
import math
import jax
import jax.numpy as jnp
from jax import lax

D = 1536
HEADS = 8
KEY = 64
VALUE = 192
TRACKS = 4096
BINS_DEV = 64
EXON_MOST = 16
BINS = 256
OUT_BINS = 512
SEQS = 4
VARIANTS = 2
GENES = 8
EXONS = 64


def draw_query_weight(key, part):
    own_part = jax.random.normal(jax.random.fold_in(key, 11), (D, HEADS * KEY), jnp.float32)
    mixed = own_part / math.sqrt(D)
    return jnp.clip(mixed, -2.0, 2.0).astype(jnp.bfloat16)


def draw_key_weight(key, part):
    own_part = jax.random.normal(jax.random.fold_in(key, 12), (D, HEADS * KEY), jnp.float32)
    mixed = own_part / math.sqrt(D)
    return jnp.clip(mixed, -2.0, 2.0).astype(jnp.bfloat16)


def exon_layout(key):
    top_start = OUT_BINS - EXON_MOST
    reach = min(4 * BINS_DEV, top_start)
    genes_drawn = jax.random.randint(jax.random.fold_in(key, 201), (VARIANTS, EXONS), 0, GENES, jnp.int32)
    every_gene = jnp.broadcast_to(jnp.arange(GENES, dtype=jnp.int32)[None, :], (VARIANTS, GENES))
    genes_all = jnp.concatenate([every_gene, genes_drawn[:, GENES:]], axis=1)
    centers = jax.random.randint(jax.random.fold_in(key, 202), (VARIANTS, GENES), 0, top_start + 1, jnp.int32)
    gene_hit = (genes_all[:, :, None] == jnp.arange(GENES, dtype=jnp.int32)[None, None, :]).astype(jnp.int32)
    exon_center = jnp.sum(gene_hit * centers[:, None, :], axis=2)
    jitter = jax.random.randint(jax.random.fold_in(key, 203), (VARIANTS, EXONS), -reach, reach + 1, jnp.int32)
    starts = jnp.clip(exon_center + jitter, 0, top_start)
    column = jnp.arange(EXONS, dtype=jnp.int32)[None, :]
    starts = jnp.where(column == 0, 0, starts)
    starts = jnp.where(column == 1, top_start, starts)
    return (genes_all, starts.astype(jnp.int32))


def draw_exon_gene(key, part):
    return exon_layout(jax.random.fold_in(key, 77))[0]


def draw_exon_start(key, part):
    return exon_layout(jax.random.fold_in(key, 77))[1]


def set_ends(entries, rng, smallest, high):
    place = [jax.random.randint(jax.random.fold_in(rng, axis), (), 0, length) for axis, length in enumerate(entries.shape)]
    main_axis = entries.shape.index(max(entries.shape))
    beside = place[:main_axis] + [(place[main_axis] + 1) % entries.shape[main_axis]] + place[main_axis + 1:]
    return entries.at[tuple(place)].set(smallest).at[tuple(beside)].set(high)


def steps_of(rng, extent, pieces, least, top_value):
    level = 1.0
    for dim, parts in pieces:
        steps = jax.random.uniform(jax.random.fold_in(jax.random.fold_in(rng, 6), dim), (parts,), jnp.float32, least / len(pieces), top_value / len(pieces))
        level = level * jnp.repeat(jnp.exp(steps), extent[dim] // parts).reshape((-1,) + (1,) * (len(extent) - 1 - dim))
    return level


def centred(rng, shape, scale, limit, shards=(), kind=jnp.bfloat16):
    gain = steps_of(rng, shape, shards, -0.22, 0.18) if shards else 1.0
    values = jax.random.normal(rng, shape, jnp.float32) * scale * gain
    return jnp.minimum(jnp.maximum(values, -limit), limit).astype(kind)


def setup_inputs(seed: int = 0, part: int = 0) -> dict:
    streams_of = jax.random.split(jax.random.key(seed), 14)
    part_keys = jax.random.split(jax.random.fold_in(streams_of[13], part), 14)
    seq_input = centred(part_keys[0], (SEQS, BINS, D), 1.0, 6.0, ((0, 4), (1, 4)))
    skip_input = centred(part_keys[1], (SEQS, OUT_BINS, D), 1.0, 6.0, ((0, 4), (1, 4)))
    norm_gain = jnp.clip(1.0 + 0.1 * jax.random.normal(streams_of[2], (D,), jnp.float32), 0.5, 1.5)
    query_weight = draw_query_weight(jax.random.fold_in(streams_of[13], 71), part)
    key_weight = draw_key_weight(jax.random.fold_in(streams_of[13], 71), part)
    value_weight = centred(streams_of[5], (D, D), D ** -0.5, 0.15625)
    conv_weight = centred(streams_of[6], (3, D), 0.6, 3.0, (), jnp.float32)
    head_weight = centred(streams_of[7], (D, TRACKS), D ** -0.5, 0.15625, ((1, 4),))
    head_bias = centred(streams_of[8], (TRACKS,), 1.0, 4.0, ((0, 4),), jnp.float32)
    exon_start = draw_exon_start(jax.random.fold_in(jax.random.fold_in(streams_of[13], part), 71), part)
    exon_length = set_ends(jax.random.randint(part_keys[10], (VARIANTS, EXONS), 1, EXON_MOST + 1), jax.random.fold_in(part_keys[10], 1), 1, EXON_MOST).astype(jnp.int32)
    exon_gene = draw_exon_gene(jax.random.fold_in(jax.random.fold_in(streams_of[13], part), 71), part)
    gene_order = jax.vmap(lambda own: jax.random.permutation(own, GENES))(jax.random.split(part_keys[12], VARIANTS)).reshape((VARIANTS, GENES)).astype(jnp.int32)
    return {"seq_input": seq_input, "skip_input": skip_input, "norm_gain": norm_gain, "query_weight": query_weight, "key_weight": key_weight, "value_weight": value_weight, "conv_weight": conv_weight, "head_weight": head_weight, "head_bias": head_bias, "exon_start": exon_start, "exon_length": exon_length, "exon_gene": exon_gene, "gene_order": gene_order}


EPSILON = 1e-05

def layer_normed(rows, norm_gain):
    rows_wide = rows.astype(jnp.float32)
    center = lax.optimization_barrier(jnp.mean(rows_wide, axis=-1, keepdims=True))
    spread_sq = lax.optimization_barrier(jnp.mean(jnp.square(rows_wide - center), axis=-1, keepdims=True))
    return ((rows_wide - center) * lax.rsqrt(spread_sq + EPSILON) * norm_gain).astype(jnp.bfloat16)

def gene_masks(exon_start, exon_length, exon_gene, gene_order, positions):
    lower = exon_start[:, :, None]
    upper = lower + exon_length[:, :, None]
    inside = ((positions[None, None, :] >= lower) & (positions[None, None, :] < upper)).astype(jnp.float32)
    chosen = (exon_gene[:, None, :] == gene_order[:, :, None]).astype(jnp.float32)
    return jnp.einsum('vpe,veb->vpb', chosen, inside, precision=lax.Precision.HIGHEST)

def reference(seq_input, skip_input, norm_gain, query_weight, key_weight, value_weight, conv_weight, head_weight, head_bias, exon_start, exon_length, exon_gene, gene_order):
    positions = jnp.arange(OUT_BINS, dtype=jnp.int32)
    seq_masks = jnp.repeat(gene_masks(exon_start, exon_length, exon_gene, gene_order, positions), 2, axis=0)
    block_rows = math.gcd(BINS, 512)

    def one_sequence(operands):
        rows, skip_rows, seq_mask = operands
        normed = layer_normed(rows, norm_gain)
        queries = jnp.dot(normed, query_weight, preferred_element_type=jnp.float32).astype(jnp.bfloat16).reshape(BINS, HEADS, KEY)
        keys_all = jnp.dot(normed, key_weight, preferred_element_type=jnp.float32).astype(jnp.bfloat16).reshape(BINS, HEADS, KEY)
        values_all = jnp.dot(normed, value_weight, preferred_element_type=jnp.float32).astype(jnp.bfloat16).reshape(BINS, HEADS, VALUE)

        def query_block(block_queries):
            logits = jnp.einsum('qhk,phk->hqp', block_queries.astype(jnp.float32), keys_all.astype(jnp.float32)) / math.sqrt(KEY)
            row_peak = lax.optimization_barrier(jnp.max(logits, axis=-1, keepdims=True))
            expo = jnp.exp(logits - row_peak)
            denom = lax.optimization_barrier(jnp.sum(expo, axis=-1))
            probs = expo.astype(jnp.bfloat16)
            mixed = jnp.einsum('hqp,phv->qhv', probs.astype(jnp.float32), values_all.astype(jnp.float32))
            mixed = mixed / jnp.transpose(denom)[:, :, None]
            return mixed.reshape(block_queries.shape[0], D)
        attention = lax.map(query_block, queries.reshape(BINS // block_rows, block_rows, HEADS, KEY)).reshape(BINS, D)
        attended = (rows.astype(jnp.float32) + attention).astype(jnp.bfloat16)
        upsampled = jnp.repeat(attended.astype(jnp.float32), 2, axis=0) + skip_rows.astype(jnp.float32)
        padded = jnp.pad(upsampled, ((1, 1), (0, 0)))
        convolved = conv_weight[0] * padded[:-2] + conv_weight[1] * padded[1:-1] + conv_weight[2] * padded[2:]
        feature = jax.nn.gelu(convolved, approximate=True).astype(jnp.bfloat16)
        predicted = jax.nn.softplus(jnp.dot(feature, head_weight, preferred_element_type=jnp.float32) + head_bias)
        return jnp.dot(seq_mask, predicted, precision=lax.Precision.HIGHEST)
    coverage = lax.map(one_sequence, (seq_input, skip_input, seq_masks))
    return jnp.log1p(coverage[1::2]) - jnp.log1p(coverage[0::2])
```

```python
import functools
import math

import jax
import jax.numpy as jnp
from jax import lax
from jax.experimental import pallas as pl
from jax.experimental.pallas import tpu as pltpu
from jax.sharding import PartitionSpec as P

HEADS = 8
KEY = 64
VALUE = 192
EPSILON = 1e-05
HALO = 16
GROUP = 2
CHUNKS = HEADS // GROUP
KCOLS = GROUP * KEY
VCOLS = GROUP * VALUE
TILE = 256
MESH = pl.DeviceIdType.MESH
BF16 = jnp.bfloat16
F32 = jnp.float32


def normalise(rows, gain):
    wide = rows.astype(F32)
    center = jnp.mean(wide, axis=-1, keepdims=True)
    spread_sq = jnp.mean(jnp.square(wide - center), axis=-1, keepdims=True)
    return ((wide - center) * lax.rsqrt(spread_sq + EPSILON) * gain).astype(BF16)


def softplus(x):
    return jnp.maximum(x, 0.0) + jnp.log1p(jnp.exp(-jnp.abs(x)))


def kernel(
    S,
    Z,
    x_ref,
    skip_ref,
    gain_ref,
    conv_ref,
    bias_ref,
    start_ref,
    length_ref,
    gene_ref,
    order_ref,
    wq_hbm,
    wk_hbm,
    wv_hbm,
    wh_hbm,
    out_ref,
    wq,
    wk,
    wv,
    wh,
    xall,
    xq,
    normed,
    normed_q,
    mixed,
    select,
    masks,
    feat,
    cover,
    landed,
    w_sem,
    x_send,
    x_recv,
    halo_send,
    halo_recv,
    up_send,
    down_send,
    f_recv,
    c_send,
    c_recv,
):
    bins, width = x_ref.shape
    out_bins = 2 * bins
    variants, exons = start_ref.shape
    genes = order_ref.shape[1]
    per_owner = genes // S
    owner_rows = Z * per_owner
    half_rows = owner_rows // 2
    tracks = wh.shape[1]
    q_rows = bins + 2 * HALO

    me = lax.axis_index("seq")
    z = lax.axis_index("pair")
    row, core = me // 2, me % 2
    sibling = row * 2 + (1 - core)
    left, right = (me + S - 1) % S, (me + 1) % S
    has_up, has_down = z < Z - 1, z > 0

    loads = [
        pltpu.make_async_copy(src, dst, w_sem.at[i])
        for i, (src, dst) in enumerate(
            ((wq_hbm, wq), (wk_hbm, wk), (wv_hbm, wv), (wh_hbm, wh))
        )
    ]
    for load in loads:
        load.start()

    barrier = pltpu.get_barrier_semaphore()
    for d in range(1, S):
        pl.semaphore_signal(barrier, inc=1, device_id={"seq": (me + d) % S}, device_id_type=MESH)

    @pl.when(has_up)
    def _():
        pl.semaphore_signal(barrier, inc=1, device_id={"pair": z + 1}, device_id_type=MESH)

    @pl.when(has_down)
    def _():
        pl.semaphore_signal(barrier, inc=1, device_id={"pair": z - 1}, device_id_type=MESH)

    line = jnp.where(has_up, 1, 0) + jnp.where(has_down, 1, 0)
    pl.semaphore_wait(barrier, S - 1 + line)

    rows_n = S // 2

    def x_copy(src, slot, sem, target):
        return pltpu.make_async_remote_copy(
            src_ref=src,
            dst_ref=xall.at[slot],
            send_sem=x_send.at[sem],
            recv_sem=x_recv.at[slot],
            device_id={"seq": target},
            device_id_type=MESH,
        )

    sends = []
    for d in range(1, rows_n):
        sends.append(x_copy(x_ref, me, d, ((row + d) % rows_n) * 2 + core))
    sends.append(x_copy(x_ref, me, 0, sibling))
    skip_low = bins + 2 * HALO
    skip_own = skip_low + HALO
    skip_high = skip_own + out_bins
    sends.append(
        pltpu.make_async_remote_copy(
            src_ref=skip_ref.at[pl.ds(0, HALO)],
            dst_ref=mixed.at[pl.ds(skip_high, HALO)],
            send_sem=halo_send.at[0],
            recv_sem=halo_recv.at[0],
            device_id={"seq": left},
            device_id_type=MESH,
        )
    )
    sends.append(
        pltpu.make_async_remote_copy(
            src_ref=skip_ref.at[pl.ds(out_bins - HALO, HALO)],
            dst_ref=mixed.at[pl.ds(skip_low, HALO)],
            send_sem=halo_send.at[1],
            recv_sem=halo_recv.at[1],
            device_id={"seq": right},
            device_id_type=MESH,
        )
    )
    halos = sends[-2:]
    for copy in sends:
        copy.start()

    gain = gain_ref[...]
    xall[me] = x_ref[...]
    mixed[skip_own:skip_high] = skip_ref[...]
    normed[me] = normalise(x_ref[...], gain)
    cover[...] = jnp.zeros_like(cover)

    pick_row = lax.broadcasted_iota(jnp.int32, (3 * out_bins, mixed.shape[0]), 0)
    pick_col = lax.broadcasted_iota(jnp.int32, (3 * out_bins, mixed.shape[0]), 1)
    offset = pick_row % out_bins + pick_row // out_bins - 1
    place = me * out_bins + offset
    chosen = (pick_col == (offset + 2 * HALO) // 2) | (pick_col == offset + skip_own)
    chosen = chosen & (place >= 0) & (place < S * out_bins)
    select[...] = jnp.where(chosen, 1.0, 0.0).astype(BF16)

    eye = lax.broadcasted_iota(jnp.int32, (exons, exons), 0) == lax.broadcasted_iota(
        jnp.int32, (exons, exons), 1
    )
    position = me * out_bins + lax.broadcasted_iota(jnp.int32, (exons, out_bins), 1)
    mask_rows = S * owner_rows
    r = lax.broadcasted_iota(jnp.int32, (mask_rows, genes), 0)
    wanted = (r // owner_rows) * per_owner + r % per_owner
    hot = wanted == lax.broadcasted_iota(jnp.int32, (mask_rows, genes), 1)
    for v in range(variants):
        starts = jnp.broadcast_to(start_ref[v : v + 1, :], (exons, exons))
        lengths = jnp.broadcast_to(length_ref[v : v + 1, :], (exons, exons))
        lower = jnp.sum(jnp.where(eye, starts, 0).astype(F32), axis=1, keepdims=True)
        extent = jnp.sum(jnp.where(eye, lengths, 0).astype(F32), axis=1, keepdims=True)
        where = position.astype(F32)
        inside = jnp.where((where >= lower) & (where < lower + extent), 1.0, 0.0).astype(BF16)
        orders = jnp.broadcast_to(order_ref[v : v + 1, :], (mask_rows, genes))
        gene = jnp.sum(jnp.where(hot, orders, 0).astype(F32), axis=1, keepdims=True)
        owned = jnp.broadcast_to(gene_ref[v : v + 1, :], (mask_rows, exons)).astype(F32)
        match = jnp.where(owned == gene, 1.0, 0.0).astype(BF16)
        masks[v] = jnp.dot(match, inside, preferred_element_type=F32)

    for d in range(1, rows_n):
        slot = ((row + rows_n - d) % rows_n) * 2 + core
        x_copy(x_ref, slot, d, sibling).wait_recv()
        forward = x_copy(xall.at[slot], slot, rows_n + d, sibling)
        forward.start()
        sends.append(forward)
        normed[slot] = normalise(xall[slot], gain)
    for d in range(rows_n):
        slot = ((row + rows_n - d) % rows_n) * 2 + (1 - core)
        x_copy(x_ref, slot, d, sibling).wait_recv()
        normed[slot] = normalise(xall[slot], gain)
    for source, target in ((xall, xq), (normed, normed_q)):
        target[0:HALO] = source[left, bins - HALO : bins]
        target[HALO : HALO + bins] = source[me]
        target[HALO + bins : q_rows] = source[right, 0:HALO]
    for halo in halos:
        halo.wait_recv()
    for load in loads[:3]:
        load.wait()

    def block_copy(block, chunk, sem, target):
        view = feat.at[block, :, pl.ds(pl.multiple_of(chunk * VCOLS, 128), VCOLS)]
        return pltpu.make_async_remote_copy(
            src_ref=view,
            dst_ref=view,
            send_sem=sem.at[block, chunk],
            recv_sem=f_recv.at[block, chunk],
            device_id={"pair": target},
            device_id_type=MESH,
        )

    def send_up(block, chunk):
        @pl.when(has_up)
        def _():
            block_copy(block, chunk, up_send, z + 1).start()

    def send_down(block, chunk):
        @pl.when(has_down)
        def _():
            block_copy(block, chunk, down_send, z - 1).start()

    def arrive(distance, chunk):
        @pl.when(z - distance >= 0)
        def _():
            block_copy(z - distance, chunk, up_send, z - 1).wait_recv()
            send_up(z - distance, chunk)

        @pl.when(z + distance < Z)
        def _():
            block_copy(z + distance, chunk, down_send, z + 1).wait_recv()
            send_down(z + distance, chunk)

    all_rows = S * bins
    inv_root = 1.0 / math.sqrt(KEY)

    def attend(chunk, carry):
        kcols = pl.ds(pl.multiple_of(chunk * KCOLS, 128), KCOLS)
        vcols = pl.ds(pl.multiple_of(chunk * VCOLS, 128), VCOLS)
        everything = normed[...].reshape(all_rows, width)
        q = jnp.dot(normed_q[...], wq[:, kcols], preferred_element_type=F32)
        k = jnp.dot(everything, wk[:, kcols], preferred_element_type=F32).astype(BF16)
        v = jnp.dot(everything, wv[:, vcols], preferred_element_type=F32).astype(BF16)
        lane = lax.broadcasted_iota(jnp.int32, (q_rows, KCOLS), 1)
        stacked = jnp.concatenate(
            [jnp.where(lane // KEY == h, q, 0.0).astype(BF16) for h in range(GROUP)], axis=0
        )
        logits = (
            lax.dot_general(stacked, k, (((1,), (1,)), ((), ())), preferred_element_type=F32)
            * inv_root
        )
        expo = jnp.exp(logits - jnp.max(logits, axis=-1, keepdims=True))
        denom = jnp.sum(expo, axis=-1, keepdims=True)
        mix = jnp.dot(expo.astype(BF16), v, preferred_element_type=F32) / denom
        column = lax.broadcasted_iota(jnp.int32, (q_rows, VCOLS), 1)
        attention = jnp.where(column < VALUE, mix[:q_rows], mix[q_rows:])
        mixed[0:q_rows, vcols] = (xq[:, vcols].astype(F32) + attention).astype(BF16)
        taps = jnp.dot(select[...], mixed[:, vcols], preferred_element_type=F32)
        weight = conv_ref[:, vcols]
        convolved = (
            weight[0:1] * taps[:out_bins]
            + weight[1:2] * taps[out_bins : 2 * out_bins]
            + weight[2:3] * taps[2 * out_bins :]
        )
        feat[z, :, vcols] = jax.nn.gelu(convolved, approximate=True).astype(BF16)
        send_up(z, chunk)
        send_down(z, chunk)

        @pl.when(chunk >= 1)
        def _():
            arrive(1, chunk - 1)

        return carry

    lax.fori_loop(0, CHUNKS, attend, 0)
    arrive(1, CHUNKS - 1)
    loads[3].wait()

    index = lax.broadcasted_iota(jnp.int32, (mask_rows, out_bins), 0) % owner_rows
    sequence = 2 * ((index % half_rows) // per_owner) + index // half_rows

    def score(block):
        mask = jnp.where(sequence == block, masks[block // 2], 0.0).astype(BF16)
        mask = jnp.concatenate([mask, mask], axis=1)

        def tile(n, carry):
            cols = pl.ds(pl.multiple_of(n * TILE, 128), TILE)
            raw = jnp.dot(feat[block], wh[:, cols], preferred_element_type=F32)
            predicted = softplus(raw + bias_ref[:, cols])
            high = predicted.astype(BF16)
            low = (predicted - high.astype(F32)).astype(BF16)
            part = jnp.dot(
                mask, jnp.concatenate([high, low], axis=0), preferred_element_type=F32
            )
            cover[:, :, cols] += part.reshape(S, owner_rows, TILE)
            return carry

        lax.fori_loop(0, tracks // TILE, tile, 0)

    score(z)

    def spread(distance, carry):
        @pl.when(distance + 1 < Z)
        def _():
            for chunk in range(CHUNKS):
                arrive(distance + 1, chunk)

        @pl.when(z - distance >= 0)
        def _():
            score(z - distance)

        @pl.when(z + distance < Z)
        def _():
            score(z + distance)

        return carry

    lax.fori_loop(1, Z, spread, 0)

    def cover_copy(src, slot, sem, target):
        return pltpu.make_async_remote_copy(
            src_ref=cover.at[src],
            dst_ref=landed.at[slot],
            send_sem=c_send.at[sem],
            recv_sem=c_recv.at[slot],
            device_id={"seq": target},
            device_id_type=MESH,
        )

    for d in range(1, S):
        target = (me + d) % S
        copy = cover_copy(target, me, d, target)
        copy.start()
        sends.append(copy)
    total = cover[me]
    for d in range(1, S):
        source = (me + S - d) % S
        cover_copy(source, source, d, source).wait_recv()
        total = total + landed[source]
    logs = jnp.log1p(total)
    scores = logs[half_rows:] - logs[:half_rows]
    for v in range(variants):
        out_ref[v] = scores[v * per_owner : (v + 1) * per_owner]

    for copy in sends:
        copy.wait_send()

    def settle(block, carry):
        for chunk in range(CHUNKS):
            @pl.when(has_up & (block <= z))
            def _():
                block_copy(block, chunk, up_send, z + 1).wait_send()

            @pl.when(has_down & (block >= z))
            def _():
                block_copy(block, chunk, down_send, z - 1).wait_send()

        return carry

    lax.fori_loop(0, Z, settle, 0)


def body(
    S,
    Z,
    seq_input,
    skip_input,
    norm_gain,
    query_weight,
    key_weight,
    value_weight,
    conv_weight,
    head_weight,
    head_bias,
    exon_start,
    exon_length,
    exon_gene,
    gene_order,
):
    bins, width = seq_input.shape[1:]
    tracks = head_weight.shape[1]
    variants = exon_start.shape[0]
    per_owner = gene_order.shape[1] // S
    owner_rows = Z * per_owner
    q_rows = bins + 2 * HALO
    mixed_rows = q_rows + 2 * bins + 2 * HALO
    vmem = pl.BlockSpec(memory_space=pltpu.VMEM)
    hbm = pl.BlockSpec(memory_space=pl.ANY)
    dma = pltpu.SemaphoreType.DMA
    return pl.pallas_call(
        functools.partial(kernel, S, Z),
        out_shape=jax.ShapeDtypeStruct((variants, per_owner, tracks), F32),
        in_specs=[vmem] * 9 + [hbm] * 4,
        out_specs=vmem,
        scratch_shapes=[
            pltpu.VMEM(query_weight.shape, BF16),
            pltpu.VMEM(key_weight.shape, BF16),
            pltpu.VMEM(value_weight.shape, BF16),
            pltpu.VMEM(head_weight.shape, BF16),
            pltpu.VMEM((S, bins, width), BF16),
            pltpu.VMEM((q_rows, width), BF16),
            pltpu.VMEM((S, bins, width), BF16),
            pltpu.VMEM((q_rows, width), BF16),
            pltpu.VMEM((mixed_rows, width), BF16),
            pltpu.VMEM((6 * bins, mixed_rows), BF16),
            pltpu.VMEM((variants, S * owner_rows, 2 * bins), F32),
            pltpu.VMEM((Z, 2 * bins, width), BF16),
            pltpu.VMEM((S, owner_rows, tracks), F32),
            pltpu.VMEM((S, owner_rows, tracks), F32),
            dma((4,)),
            dma((S,)),
            dma((S,)),
            dma((2,)),
            dma((2,)),
            dma((Z, CHUNKS)),
            dma((Z, CHUNKS)),
            dma((Z, CHUNKS)),
            dma((S,)),
            dma((S,)),
        ],
        compiler_params=pltpu.CompilerParams(
            collective_id=0, has_side_effects=True, vmem_limit_bytes=56 * 1024 * 1024
        ),
    )(
        seq_input[0],
        skip_input[0],
        norm_gain[None],
        conv_weight,
        head_bias[None],
        exon_start,
        exon_length,
        exon_gene,
        gene_order,
        query_weight,
        key_weight,
        value_weight,
        head_weight,
    )


def solution(mesh):
    placed = (
        P(("grp", "pair"), "seq", None),
        P(("grp", "pair"), "seq", None),
        P(),
        P(),
        P(),
        P(),
        P(),
        P(None, "pair"),
        P("pair"),
        P("grp", None),
        P("grp", None),
        P("grp", None),
        P("grp", None),
    )
    return jax.shard_map(
        functools.partial(body, mesh.shape["seq"], mesh.shape["pair"]),
        mesh=mesh,
        in_specs=placed,
        out_specs=P("grp", "seq", "pair"),
        check_vma=False,
    )
```

```python
import functools
import math

import jax
import jax.numpy as jnp
from jax import lax
from jax.experimental import pallas as pl
from jax.experimental.pallas import tpu as pltpu
from jax.sharding import PartitionSpec as P

HEADS = 8
KEY = 64
VALUE = 192
EPSILON = 1e-05
HALO = 16
GROUP = 2
CHUNKS = HEADS // GROUP
KCOLS = GROUP * KEY
VCOLS = GROUP * VALUE
TILE = 256
PARTS = 2
MESH = pl.DeviceIdType.MESH
BF16 = jnp.bfloat16
F32 = jnp.float32


def normalise(rows, gain):
    wide = rows.astype(F32)
    center = jnp.mean(wide, axis=-1, keepdims=True)
    spread_sq = jnp.mean(jnp.square(wide - center), axis=-1, keepdims=True)
    return ((wide - center) * lax.rsqrt(spread_sq + EPSILON) * gain).astype(BF16)


def softplus(x):
    return jnp.maximum(x, 0.0) + jnp.log1p(jnp.exp(-jnp.abs(x)))


def kernel(
    S,
    Z,
    x_hbm,
    skip_hbm,
    gain_ref,
    conv_ref,
    bias_ref,
    start_ref,
    length_ref,
    gene_ref,
    order_ref,
    wq_hbm,
    wk_hbm,
    wv_hbm,
    wh_hbm,
    out_ref,
    wq,
    wk,
    wv,
    wh,
    xall,
    xq,
    normed,
    normed_q,
    mixed,
    select,
    masks,
    feat,
    raw,
    cover,
    landed,
    w_sem,
    x_send,
    x_recv,
    halo_send,
    halo_recv,
    up_send,
    down_send,
    f_recv,
    c_send,
    c_recv,
):
    bins, width = x_hbm.shape
    out_bins = 2 * bins
    variants, exons = start_ref.shape
    genes = order_ref.shape[1]
    per_owner = genes // S
    owner_rows = Z * per_owner
    half_rows = owner_rows // 2
    tracks = wh.shape[1]
    q_rows = bins + 2 * HALO

    me = lax.axis_index("seq")
    z = lax.axis_index("pair")
    row, core = me // 2, me % 2
    sibling = row * 2 + (1 - core)
    left, right = (me + S - 1) % S, (me + 1) % S
    has_up, has_down = z < Z - 1, z > 0

    skip_low = bins + 2 * HALO
    skip_own = skip_low + HALO
    skip_high = skip_own + out_bins
    loads = [
        pltpu.make_async_copy(src, dst, w_sem.at[i])
        for i, (src, dst) in enumerate(
            (
                (x_hbm, xall.at[me]),
                (skip_hbm, mixed.at[pl.ds(skip_own, out_bins)]),
                (wk_hbm, wk),
                (wv_hbm, wv),
                (wq_hbm, wq),
                (wh_hbm, wh),
            )
        )
    ]
    loads[0].start()

    barrier = pltpu.get_barrier_semaphore()
    for d in range(1, S):
        pl.semaphore_signal(barrier, inc=1, device_id={"seq": (me + d) % S}, device_id_type=MESH)

    @pl.when(has_up)
    def _():
        pl.semaphore_signal(barrier, inc=1, device_id={"pair": z + 1}, device_id_type=MESH)

    @pl.when(has_down)
    def _():
        pl.semaphore_signal(barrier, inc=1, device_id={"pair": z - 1}, device_id_type=MESH)

    line = jnp.where(has_up, 1, 0) + jnp.where(has_down, 1, 0)
    pl.semaphore_wait(barrier, S - 1 + line)

    rows_n = S // 2

    part_rows = bins // PARTS

    def x_copy(src, slot, part, sem, target):
        piece = pl.ds(part * part_rows, part_rows)
        return pltpu.make_async_remote_copy(
            src_ref=src.at[piece],
            dst_ref=xall.at[slot, piece],
            send_sem=x_send.at[sem, part],
            recv_sem=x_recv.at[slot, part],
            device_id={"seq": target},
            device_id_type=MESH,
        )

    sends = []
    for part in range(PARTS):
        for d in range(1, rows_n):
            sends.append(x_copy(x_hbm, me, part, d, ((row + d) % rows_n) * 2 + core))
    for part in range(PARTS):
        sends.append(x_copy(x_hbm, me, part, 0, sibling))
    sends.append(
        pltpu.make_async_remote_copy(
            src_ref=skip_hbm.at[pl.ds(0, HALO)],
            dst_ref=mixed.at[pl.ds(skip_high, HALO)],
            send_sem=halo_send.at[0],
            recv_sem=halo_recv.at[0],
            device_id={"seq": left},
            device_id_type=MESH,
        )
    )
    sends.append(
        pltpu.make_async_remote_copy(
            src_ref=skip_hbm.at[pl.ds(out_bins - HALO, HALO)],
            dst_ref=mixed.at[pl.ds(skip_low, HALO)],
            send_sem=halo_send.at[1],
            recv_sem=halo_recv.at[1],
            device_id={"seq": right},
            device_id_type=MESH,
        )
    )
    halos = sends[-2:]
    for copy in sends:
        copy.start()
    for load in loads[1:]:
        load.start()

    gain = gain_ref[...].reshape(1, width)
    loads[0].wait()
    normed[me] = normalise(xall[me], gain)
    cover[...] = jnp.zeros_like(cover)

    pick_row = lax.broadcasted_iota(jnp.int32, (3 * out_bins, mixed.shape[0]), 0)
    pick_col = lax.broadcasted_iota(jnp.int32, (3 * out_bins, mixed.shape[0]), 1)
    offset = pick_row % out_bins + pick_row // out_bins - 1
    place = me * out_bins + offset
    chosen = (pick_col == (offset + 2 * HALO) // 2) | (pick_col == offset + skip_own)
    chosen = chosen & (place >= 0) & (place < S * out_bins)
    select[...] = jnp.where(chosen, 1.0, 0.0).astype(BF16)

    eye = lax.broadcasted_iota(jnp.int32, (exons, exons), 0) == lax.broadcasted_iota(
        jnp.int32, (exons, exons), 1
    )
    position = me * out_bins + lax.broadcasted_iota(jnp.int32, (exons, out_bins), 1)
    mask_rows = S * owner_rows
    r = lax.broadcasted_iota(jnp.int32, (mask_rows, genes), 0)
    wanted = (r // owner_rows) * per_owner + r % per_owner
    hot = wanted == lax.broadcasted_iota(jnp.int32, (mask_rows, genes), 1)
    for v in range(variants):
        starts = jnp.broadcast_to(start_ref[v : v + 1, :], (exons, exons))
        lengths = jnp.broadcast_to(length_ref[v : v + 1, :], (exons, exons))
        lower = jnp.sum(jnp.where(eye, starts, 0).astype(F32), axis=1, keepdims=True)
        extent = jnp.sum(jnp.where(eye, lengths, 0).astype(F32), axis=1, keepdims=True)
        where = position.astype(F32)
        inside = jnp.where((where >= lower) & (where < lower + extent), 1.0, 0.0).astype(BF16)
        orders = jnp.broadcast_to(order_ref[v : v + 1, :], (mask_rows, genes))
        gene = jnp.sum(jnp.where(hot, orders, 0).astype(F32), axis=1, keepdims=True)
        owned = jnp.broadcast_to(gene_ref[v : v + 1, :], (mask_rows, exons)).astype(F32)
        match = jnp.where(owned == gene, 1.0, 0.0).astype(BF16)
        masks[v] = jnp.dot(match, inside, preferred_element_type=F32)

    for part in range(PARTS):
        for d in range(1, rows_n):
            slot = ((row + rows_n - d) % rows_n) * 2 + core
            x_copy(x_hbm, slot, part, d, sibling).wait_recv()
            forward = x_copy(xall.at[slot], slot, part, rows_n + d, sibling)
            forward.start()
            sends.append(forward)
            piece = pl.ds(part * part_rows, part_rows)
            normed[slot, piece] = normalise(xall[slot, piece], gain)
    for d in range(rows_n):
        slot = ((row + rows_n - d) % rows_n) * 2 + (1 - core)
        for part in range(PARTS):
            x_copy(x_hbm, slot, part, d, sibling).wait_recv()
            piece = pl.ds(part * part_rows, part_rows)
            normed[slot, piece] = normalise(xall[slot, piece], gain)
    for source, target in ((xall, xq), (normed, normed_q)):
        target[0:HALO] = source[left, bins - HALO : bins]
        target[HALO : HALO + bins] = source[me]
        target[HALO + bins : q_rows] = source[right, 0:HALO]
    for halo in halos:
        halo.wait_recv()
    for load in loads[1:5]:
        load.wait()

    def block_copy(block, chunk, sem, target):
        view = feat.at[block, :, pl.ds(pl.multiple_of(chunk * VCOLS, 128), VCOLS)]
        return pltpu.make_async_remote_copy(
            src_ref=view,
            dst_ref=view,
            send_sem=sem.at[block, chunk],
            recv_sem=f_recv.at[block, chunk],
            device_id={"pair": target},
            device_id_type=MESH,
        )

    def send_up(block, chunk):
        @pl.when(has_up)
        def _():
            block_copy(block, chunk, up_send, z + 1).start()

    def send_down(block, chunk):
        @pl.when(has_down)
        def _():
            block_copy(block, chunk, down_send, z - 1).start()

    def relay(distance, chunk):
        @pl.when(has_up & (z - distance >= 0))
        def _():
            block_copy(z - distance, chunk, up_send, z - 1).wait_recv()
            send_up(z - distance, chunk)

        @pl.when(has_down & (z + distance < Z))
        def _():
            block_copy(z + distance, chunk, down_send, z + 1).wait_recv()
            send_down(z + distance, chunk)

    def arrive(block, chunk):
        @pl.when((block < z) & jnp.logical_not(has_up))
        def _():
            block_copy(block, chunk, up_send, z - 1).wait_recv()

        @pl.when((block > z) & jnp.logical_not(has_down))
        def _():
            block_copy(block, chunk, down_send, z + 1).wait_recv()

    all_rows = S * bins
    inv_root = 1.0 / math.sqrt(KEY)

    def attend(chunk, carry):
        kcols = pl.ds(pl.multiple_of(chunk * KCOLS, 128), KCOLS)
        vcols = pl.ds(pl.multiple_of(chunk * VCOLS, 128), VCOLS)
        everything = normed[...].reshape(all_rows, width)
        q = jnp.dot(normed_q[...], wq[:, kcols], preferred_element_type=F32)
        k = jnp.dot(everything, wk[:, kcols], preferred_element_type=F32).astype(BF16)
        v = jnp.dot(everything, wv[:, vcols], preferred_element_type=F32).astype(BF16)
        lane = lax.broadcasted_iota(jnp.int32, (q_rows, KCOLS), 1)
        stacked = jnp.concatenate(
            [jnp.where(lane // KEY == h, q, 0.0).astype(BF16) for h in range(GROUP)], axis=0
        )
        logits = (
            lax.dot_general(stacked, k, (((1,), (1,)), ((), ())), preferred_element_type=F32)
            * inv_root
        )
        expo = jnp.exp(logits - jnp.max(logits, axis=-1, keepdims=True))
        denom = jnp.sum(expo, axis=-1, keepdims=True)
        mix = jnp.dot(expo.astype(BF16), v, preferred_element_type=F32) / denom
        column = lax.broadcasted_iota(jnp.int32, (q_rows, VCOLS), 1)
        attention = jnp.where(column < VALUE, mix[:q_rows], mix[q_rows:])
        mixed[0:q_rows, vcols] = (xq[:, vcols].astype(F32) + attention).astype(BF16)
        taps = jnp.dot(select[...], mixed[:, vcols], preferred_element_type=F32)
        weight = conv_ref[:, vcols]
        convolved = (
            weight[0:1] * taps[:out_bins]
            + weight[1:2] * taps[out_bins : 2 * out_bins]
            + weight[2:3] * taps[2 * out_bins :]
        )
        feat[z, :, vcols] = jax.nn.gelu(convolved, approximate=True).astype(BF16)
        send_up(z, chunk)
        send_down(z, chunk)

        @pl.when(chunk >= 1)
        def _():
            relay(1, chunk - 1)

        return carry

    lax.fori_loop(0, CHUNKS, attend, 0)
    relay(1, CHUNKS - 1)
    loads[5].wait()

    index = lax.broadcasted_iota(jnp.int32, (mask_rows, out_bins), 0) % owner_rows
    sequence = 2 * ((index % half_rows) // per_owner) + index // half_rows

    early = (CHUNKS - 1) * VCOLS

    def score(block):
        mask = jnp.where(sequence == block, masks[block // 2], 0.0).astype(BF16)
        mask = jnp.concatenate([mask, mask], axis=1)

        for chunk in range(CHUNKS - 1):
            arrive(block, chunk)

        def first(n, carry):
            cols = pl.ds(pl.multiple_of(n * TILE, 128), TILE)
            raw[:, cols] = bias_ref[:, cols] + jnp.dot(
                feat[block, :, :early], wh[:early, cols], preferred_element_type=F32
            )
            return carry

        lax.fori_loop(0, tracks // TILE, first, 0)
        arrive(block, CHUNKS - 1)

        def second(n, carry):
            cols = pl.ds(pl.multiple_of(n * TILE, 128), TILE)
            predicted = softplus(
                raw[:, cols]
                + jnp.dot(feat[block, :, early:], wh[early:, cols], preferred_element_type=F32)
            )
            high = predicted.astype(BF16)
            low = (predicted - high.astype(F32)).astype(BF16)
            part = jnp.dot(
                mask, jnp.concatenate([high, low], axis=0), preferred_element_type=F32
            )
            cover[:, :, cols] += part.reshape(S, owner_rows, TILE)
            return carry

        lax.fori_loop(0, tracks // TILE, second, 0)

    score(z)

    def spread(distance, carry):
        @pl.when(distance + 1 < Z)
        def _():
            for chunk in range(CHUNKS):
                relay(distance + 1, chunk)

        @pl.when(z - distance >= 0)
        def _():
            score(z - distance)

        @pl.when(z + distance < Z)
        def _():
            score(z + distance)

        return carry

    lax.fori_loop(1, Z, spread, 0)

    def cover_copy(src, slot, sem, target):
        return pltpu.make_async_remote_copy(
            src_ref=cover.at[src],
            dst_ref=landed.at[slot],
            send_sem=c_send.at[sem],
            recv_sem=c_recv.at[slot],
            device_id={"seq": target},
            device_id_type=MESH,
        )

    for d in range(1, S):
        target = (me + d) % S
        copy = cover_copy(target, me, d, target)
        copy.start()
        sends.append(copy)
    total = cover[me]
    for d in range(1, S):
        source = (me + S - d) % S
        cover_copy(source, source, d, source).wait_recv()
        total = total + landed[source]
    logs = jnp.log1p(total)
    scores = logs[half_rows:] - logs[:half_rows]
    for v in range(variants):
        out_ref[v] = scores[v * per_owner : (v + 1) * per_owner]

    for copy in sends:
        copy.wait_send()

    def settle(block, carry):
        for chunk in range(CHUNKS):
            @pl.when(has_up & (block <= z))
            def _():
                block_copy(block, chunk, up_send, z + 1).wait_send()

            @pl.when(has_down & (block >= z))
            def _():
                block_copy(block, chunk, down_send, z - 1).wait_send()

        return carry

    lax.fori_loop(0, Z, settle, 0)


def body(
    S,
    Z,
    seq_input,
    skip_input,
    norm_gain,
    query_weight,
    key_weight,
    value_weight,
    conv_weight,
    head_weight,
    head_bias,
    exon_start,
    exon_length,
    exon_gene,
    gene_order,
):
    bins, width = seq_input.shape[1:]
    tracks = head_weight.shape[1]
    variants = exon_start.shape[0]
    per_owner = gene_order.shape[1] // S
    owner_rows = Z * per_owner
    q_rows = bins + 2 * HALO
    mixed_rows = q_rows + 2 * bins + 2 * HALO
    vmem = pl.BlockSpec(memory_space=pltpu.VMEM)
    hbm = pl.BlockSpec(memory_space=pl.ANY)
    dma = pltpu.SemaphoreType.DMA
    return pl.pallas_call(
        functools.partial(kernel, S, Z),
        out_shape=jax.ShapeDtypeStruct((variants, per_owner, tracks), F32),
        in_specs=[hbm] * 2 + [vmem] * 7 + [hbm] * 4,
        out_specs=vmem,
        scratch_shapes=[
            pltpu.VMEM(query_weight.shape, BF16),
            pltpu.VMEM(key_weight.shape, BF16),
            pltpu.VMEM(value_weight.shape, BF16),
            pltpu.VMEM(head_weight.shape, BF16),
            pltpu.VMEM((S, bins, width), BF16),
            pltpu.VMEM((q_rows, width), BF16),
            pltpu.VMEM((S, bins, width), BF16),
            pltpu.VMEM((q_rows, width), BF16),
            pltpu.VMEM((mixed_rows, width), BF16),
            pltpu.VMEM((6 * bins, mixed_rows), BF16),
            pltpu.VMEM((variants, S * owner_rows, 2 * bins), F32),
            pltpu.VMEM((Z, 2 * bins, width), BF16),
            pltpu.VMEM((2 * bins, tracks), F32),
            pltpu.VMEM((S, owner_rows, tracks), F32),
            pltpu.VMEM((S, owner_rows, tracks), F32),
            dma((6,)),
            dma((S, PARTS)),
            dma((S, PARTS)),
            dma((2,)),
            dma((2,)),
            dma((Z, CHUNKS)),
            dma((Z, CHUNKS)),
            dma((Z, CHUNKS)),
            dma((S,)),
            dma((S,)),
        ],
        compiler_params=pltpu.CompilerParams(
            collective_id=0, has_side_effects=True, vmem_limit_bytes=56 * 1024 * 1024
        ),
    )(
        seq_input[0],
        skip_input[0],
        norm_gain,
        conv_weight,
        head_bias[None],
        exon_start,
        exon_length,
        exon_gene,
        gene_order,
        query_weight,
        key_weight,
        value_weight,
        head_weight,
    )


def solution(mesh):
    placed = (
        P(("grp", "pair"), "seq", None),
        P(("grp", "pair"), "seq", None),
        P(),
        P(),
        P(),
        P(),
        P(),
        P(None, "pair"),
        P("pair"),
        P("grp", None),
        P("grp", None),
        P("grp", None),
        P("grp", None),
    )
    return jax.shard_map(
        functools.partial(body, mesh.shape["seq"], mesh.shape["pair"]),
        mesh=mesh,
        in_specs=placed,
        out_specs=P("grp", "seq", "pair"),
        check_vma=False,
    )
```

```python
import functools
import math

import jax
import jax.numpy as jnp
from jax import lax
from jax.experimental import pallas as pl
from jax.experimental.pallas import tpu as pltpu
from jax.sharding import PartitionSpec as P

HEADS = 8
KEY = 64
VALUE = 192
EPSILON = 1e-05
HALO = 16
GROUP = 2
CHUNKS = HEADS // GROUP
KCOLS = GROUP * KEY
VCOLS = GROUP * VALUE
TILE = 512
PARTS = 2
MESH = pl.DeviceIdType.MESH
BF16 = jnp.bfloat16
F32 = jnp.float32


def normalise(rows, gain):
    wide = rows.astype(F32)
    center = jnp.mean(wide, axis=-1, keepdims=True)
    spread_sq = jnp.mean(jnp.square(wide - center), axis=-1, keepdims=True)
    return ((wide - center) * lax.rsqrt(spread_sq + EPSILON) * gain).astype(BF16)


def softplus(x):
    return jnp.maximum(x, 0.0) + jnp.log1p(jnp.exp(-jnp.abs(x)))


def kernel(
    S,
    Z,
    x_hbm,
    skip_hbm,
    gain_ref,
    conv_ref,
    bias_ref,
    start_ref,
    length_ref,
    gene_ref,
    order_ref,
    wq_hbm,
    wk_hbm,
    wv_hbm,
    wh_hbm,
    out_ref,
    wq,
    wk,
    wv,
    wh,
    xall,
    xq,
    normed,
    normed_q,
    mixed,
    select,
    masks,
    feat,
    raw,
    cover,
    landed,
    w_sem,
    x_send,
    x_recv,
    halo_send,
    halo_recv,
    up_send,
    down_send,
    f_recv,
    c_send,
    c_recv,
):
    bins, width = x_hbm.shape
    out_bins = 2 * bins
    variants, exons = start_ref.shape
    genes = order_ref.shape[1]
    per_owner = genes // S
    owner_rows = Z * per_owner
    half_rows = owner_rows // 2
    tracks = wh.shape[1]
    q_rows = bins + 2 * HALO

    me = lax.axis_index("seq")
    z = lax.axis_index("pair")
    row, core = me // 2, me % 2
    sibling = row * 2 + (1 - core)
    left, right = (me + S - 1) % S, (me + 1) % S
    has_up, has_down = z < Z - 1, z > 0

    skip_low = bins + 2 * HALO
    skip_own = skip_low + HALO
    skip_high = skip_own + out_bins
    loads = [
        pltpu.make_async_copy(src, dst, w_sem.at[i])
        for i, (src, dst) in enumerate(
            (
                (x_hbm, xall.at[me]),
                (skip_hbm, mixed.at[pl.ds(skip_own, out_bins)]),
                (wk_hbm, wk),
                (wv_hbm, wv),
                (wq_hbm, wq),
                (wh_hbm, wh),
            )
        )
    ]
    loads[0].start()

    barrier = pltpu.get_barrier_semaphore()
    for d in range(1, S):
        pl.semaphore_signal(barrier, inc=1, device_id={"seq": (me + d) % S}, device_id_type=MESH)

    @pl.when(has_up)
    def _():
        pl.semaphore_signal(barrier, inc=1, device_id={"pair": z + 1}, device_id_type=MESH)

    @pl.when(has_down)
    def _():
        pl.semaphore_signal(barrier, inc=1, device_id={"pair": z - 1}, device_id_type=MESH)

    line = jnp.where(has_up, 1, 0) + jnp.where(has_down, 1, 0)
    pl.semaphore_wait(barrier, S - 1 + line)

    rows_n = S // 2

    part_rows = bins // PARTS

    def x_copy(src, slot, part, sem, target):
        piece = pl.ds(part * part_rows, part_rows)
        return pltpu.make_async_remote_copy(
            src_ref=src.at[piece],
            dst_ref=xall.at[slot, piece],
            send_sem=x_send.at[sem, part],
            recv_sem=x_recv.at[slot, part],
            device_id={"seq": target},
            device_id_type=MESH,
        )

    sends = []
    for part in range(PARTS):
        for d in range(1, rows_n):
            sends.append(x_copy(x_hbm, me, part, d, ((row + d) % rows_n) * 2 + core))
    for part in range(PARTS):
        sends.append(x_copy(x_hbm, me, part, 0, sibling))
    sends.append(
        pltpu.make_async_remote_copy(
            src_ref=skip_hbm.at[pl.ds(0, HALO)],
            dst_ref=mixed.at[pl.ds(skip_high, HALO)],
            send_sem=halo_send.at[0],
            recv_sem=halo_recv.at[0],
            device_id={"seq": left},
            device_id_type=MESH,
        )
    )
    sends.append(
        pltpu.make_async_remote_copy(
            src_ref=skip_hbm.at[pl.ds(out_bins - HALO, HALO)],
            dst_ref=mixed.at[pl.ds(skip_low, HALO)],
            send_sem=halo_send.at[1],
            recv_sem=halo_recv.at[1],
            device_id={"seq": right},
            device_id_type=MESH,
        )
    )
    halos = sends[-2:]
    for copy in sends:
        copy.start()
    for load in loads[1:]:
        load.start()

    gain = gain_ref[...].reshape(1, width)
    loads[0].wait()
    normed[me] = normalise(xall[me], gain)
    cover[...] = jnp.zeros_like(cover)

    pick_row = lax.broadcasted_iota(jnp.int32, (3 * out_bins, mixed.shape[0]), 0)
    pick_col = lax.broadcasted_iota(jnp.int32, (3 * out_bins, mixed.shape[0]), 1)
    offset = pick_row % out_bins + pick_row // out_bins - 1
    place = me * out_bins + offset
    chosen = (pick_col == (offset + 2 * HALO) // 2) | (pick_col == offset + skip_own)
    chosen = chosen & (place >= 0) & (place < S * out_bins)
    select[...] = jnp.where(chosen, 1.0, 0.0).astype(BF16)

    eye = lax.broadcasted_iota(jnp.int32, (exons, exons), 0) == lax.broadcasted_iota(
        jnp.int32, (exons, exons), 1
    )
    position = me * out_bins + lax.broadcasted_iota(jnp.int32, (exons, out_bins), 1)
    mask_rows = S * owner_rows
    r = lax.broadcasted_iota(jnp.int32, (mask_rows, genes), 0)
    wanted = (r // owner_rows) * per_owner + r % per_owner
    hot = wanted == lax.broadcasted_iota(jnp.int32, (mask_rows, genes), 1)
    for v in range(variants):
        starts = jnp.broadcast_to(start_ref[v : v + 1, :], (exons, exons))
        lengths = jnp.broadcast_to(length_ref[v : v + 1, :], (exons, exons))
        lower = jnp.sum(jnp.where(eye, starts, 0).astype(F32), axis=1, keepdims=True)
        extent = jnp.sum(jnp.where(eye, lengths, 0).astype(F32), axis=1, keepdims=True)
        where = position.astype(F32)
        inside = jnp.where((where >= lower) & (where < lower + extent), 1.0, 0.0).astype(BF16)
        orders = jnp.broadcast_to(order_ref[v : v + 1, :], (mask_rows, genes))
        gene = jnp.sum(jnp.where(hot, orders, 0).astype(F32), axis=1, keepdims=True)
        owned = jnp.broadcast_to(gene_ref[v : v + 1, :], (mask_rows, exons)).astype(F32)
        match = jnp.where(owned == gene, 1.0, 0.0).astype(BF16)
        masks[v] = jnp.dot(match, inside, preferred_element_type=F32)

    for part in range(PARTS):
        for d in range(1, rows_n):
            slot = ((row + rows_n - d) % rows_n) * 2 + core
            x_copy(x_hbm, slot, part, d, sibling).wait_recv()
            forward = x_copy(xall.at[slot], slot, part, rows_n + d, sibling)
            forward.start()
            sends.append(forward)
            piece = pl.ds(part * part_rows, part_rows)
            normed[slot, piece] = normalise(xall[slot, piece], gain)
    for d in range(rows_n):
        slot = ((row + rows_n - d) % rows_n) * 2 + (1 - core)
        for part in range(PARTS):
            x_copy(x_hbm, slot, part, d, sibling).wait_recv()
            piece = pl.ds(part * part_rows, part_rows)
            normed[slot, piece] = normalise(xall[slot, piece], gain)
    for source, target in ((xall, xq), (normed, normed_q)):
        target[0:HALO] = source[left, bins - HALO : bins]
        target[HALO : HALO + bins] = source[me]
        target[HALO + bins : q_rows] = source[right, 0:HALO]
    for halo in halos:
        halo.wait_recv()
    for load in loads[1:5]:
        load.wait()

    def block_copy(block, chunk, sem, target):
        view = feat.at[block, :, pl.ds(pl.multiple_of(chunk * VCOLS, 128), VCOLS)]
        return pltpu.make_async_remote_copy(
            src_ref=view,
            dst_ref=view,
            send_sem=sem.at[block, chunk],
            recv_sem=f_recv.at[block, chunk],
            device_id={"pair": target},
            device_id_type=MESH,
        )

    def send_up(block, chunk):
        @pl.when(has_up)
        def _():
            block_copy(block, chunk, up_send, z + 1).start()

    def send_down(block, chunk):
        @pl.when(has_down)
        def _():
            block_copy(block, chunk, down_send, z - 1).start()

    def relay(distance, chunk):
        @pl.when(has_up & (z - distance >= 0))
        def _():
            block_copy(z - distance, chunk, up_send, z - 1).wait_recv()
            send_up(z - distance, chunk)

        @pl.when(has_down & (z + distance < Z))
        def _():
            block_copy(z + distance, chunk, down_send, z + 1).wait_recv()
            send_down(z + distance, chunk)

    def arrive(block, chunk):
        @pl.when((block < z) & jnp.logical_not(has_up))
        def _():
            block_copy(block, chunk, up_send, z - 1).wait_recv()

        @pl.when((block > z) & jnp.logical_not(has_down))
        def _():
            block_copy(block, chunk, down_send, z + 1).wait_recv()

    all_rows = S * bins
    inv_root = 1.0 / math.sqrt(KEY)

    def attend(chunk, carry):
        kcols = pl.ds(pl.multiple_of(chunk * KCOLS, 128), KCOLS)
        vcols = pl.ds(pl.multiple_of(chunk * VCOLS, 128), VCOLS)
        everything = normed[...].reshape(all_rows, width)
        q = jnp.dot(normed_q[...], wq[:, kcols], preferred_element_type=F32)
        k = jnp.dot(everything, wk[:, kcols], preferred_element_type=F32).astype(BF16)
        v = jnp.dot(everything, wv[:, vcols], preferred_element_type=F32).astype(BF16)
        lane = lax.broadcasted_iota(jnp.int32, (q_rows, KCOLS), 1)
        stacked = jnp.concatenate(
            [jnp.where(lane // KEY == h, q, 0.0).astype(BF16) for h in range(GROUP)], axis=0
        )
        logits = (
            lax.dot_general(stacked, k, (((1,), (1,)), ((), ())), preferred_element_type=F32)
            * inv_root
        )
        expo = jnp.exp(logits - jnp.max(logits, axis=-1, keepdims=True))
        denom = jnp.sum(expo, axis=-1, keepdims=True)
        mix = jnp.dot(expo.astype(BF16), v, preferred_element_type=F32) / denom
        column = lax.broadcasted_iota(jnp.int32, (q_rows, VCOLS), 1)
        attention = jnp.where(column < VALUE, mix[:q_rows], mix[q_rows:])
        mixed[0:q_rows, vcols] = (xq[:, vcols].astype(F32) + attention).astype(BF16)
        taps = jnp.dot(select[...], mixed[:, vcols], preferred_element_type=F32)
        weight = conv_ref[:, vcols]
        convolved = (
            weight[0:1] * taps[:out_bins]
            + weight[1:2] * taps[out_bins : 2 * out_bins]
            + weight[2:3] * taps[2 * out_bins :]
        )
        feat[z, :, vcols] = jax.nn.gelu(convolved, approximate=True).astype(BF16)
        send_up(z, chunk)
        send_down(z, chunk)

        @pl.when(chunk >= 1)
        def _():
            relay(1, chunk - 1)

        return carry

    lax.fori_loop(0, CHUNKS, attend, 0, unroll=True)
    relay(1, CHUNKS - 1)
    loads[5].wait()

    index = lax.broadcasted_iota(jnp.int32, (mask_rows, out_bins), 0) % owner_rows
    sequence = 2 * ((index % half_rows) // per_owner) + index // half_rows

    early = (CHUNKS - 1) * VCOLS

    def score(block):
        mask = jnp.where(sequence == block, masks[block // 2], 0.0).astype(BF16)
        mask = jnp.concatenate([mask, mask], axis=1)

        for chunk in range(CHUNKS - 1):
            arrive(block, chunk)

        def first(n, carry):
            cols = pl.ds(pl.multiple_of(n * TILE, 128), TILE)
            raw[:, cols] = bias_ref[:, cols] + jnp.dot(
                feat[block, :, :early], wh[:early, cols], preferred_element_type=F32
            )
            return carry

        lax.fori_loop(0, tracks // TILE, first, 0)
        arrive(block, CHUNKS - 1)

        def second(n, carry):
            cols = pl.ds(pl.multiple_of(n * TILE, 128), TILE)
            predicted = softplus(
                raw[:, cols]
                + jnp.dot(feat[block, :, early:], wh[early:, cols], preferred_element_type=F32)
            )
            high = predicted.astype(BF16)
            low = (predicted - high.astype(F32)).astype(BF16)
            part = jnp.dot(
                mask, jnp.concatenate([high, low], axis=0), preferred_element_type=F32
            )
            cover[:, :, cols] += part.reshape(S, owner_rows, TILE)
            return carry

        lax.fori_loop(0, tracks // TILE, second, 0)

    score(z)

    def spread(distance, carry):
        @pl.when(distance + 1 < Z)
        def _():
            for chunk in range(CHUNKS):
                relay(distance + 1, chunk)

        @pl.when(z - distance >= 0)
        def _():
            score(z - distance)

        @pl.when(z + distance < Z)
        def _():
            score(z + distance)

        return carry

    lax.fori_loop(1, Z, spread, 0)

    def cover_copy(src, slot, sem, target):
        return pltpu.make_async_remote_copy(
            src_ref=cover.at[src],
            dst_ref=landed.at[slot],
            send_sem=c_send.at[sem],
            recv_sem=c_recv.at[slot],
            device_id={"seq": target},
            device_id_type=MESH,
        )

    for d in range(1, S):
        target = (me + d) % S
        copy = cover_copy(target, me, d, target)
        copy.start()
        sends.append(copy)
    total = cover[me]
    for d in range(1, S):
        source = (me + S - d) % S
        cover_copy(source, source, d, source).wait_recv()
        total = total + landed[source]
    logs = jnp.log1p(total)
    scores = logs[half_rows:] - logs[:half_rows]
    for v in range(variants):
        out_ref[v] = scores[v * per_owner : (v + 1) * per_owner]

    for copy in sends:
        copy.wait_send()

    def settle(block, carry):
        for chunk in range(CHUNKS):
            @pl.when(has_up & (block <= z))
            def _():
                block_copy(block, chunk, up_send, z + 1).wait_send()

            @pl.when(has_down & (block >= z))
            def _():
                block_copy(block, chunk, down_send, z - 1).wait_send()

        return carry

    lax.fori_loop(0, Z, settle, 0)


def body(
    S,
    Z,
    seq_input,
    skip_input,
    norm_gain,
    query_weight,
    key_weight,
    value_weight,
    conv_weight,
    head_weight,
    head_bias,
    exon_start,
    exon_length,
    exon_gene,
    gene_order,
):
    bins, width = seq_input.shape[1:]
    tracks = head_weight.shape[1]
    variants = exon_start.shape[0]
    per_owner = gene_order.shape[1] // S
    owner_rows = Z * per_owner
    q_rows = bins + 2 * HALO
    mixed_rows = q_rows + 2 * bins + 2 * HALO
    vmem = pl.BlockSpec(memory_space=pltpu.VMEM)
    hbm = pl.BlockSpec(memory_space=pl.ANY)
    dma = pltpu.SemaphoreType.DMA
    return pl.pallas_call(
        functools.partial(kernel, S, Z),
        out_shape=jax.ShapeDtypeStruct((variants, per_owner, tracks), F32),
        in_specs=[hbm] * 2 + [vmem] * 7 + [hbm] * 4,
        out_specs=vmem,
        scratch_shapes=[
            pltpu.VMEM(query_weight.shape, BF16),
            pltpu.VMEM(key_weight.shape, BF16),
            pltpu.VMEM(value_weight.shape, BF16),
            pltpu.VMEM(head_weight.shape, BF16),
            pltpu.VMEM((S, bins, width), BF16),
            pltpu.VMEM((q_rows, width), BF16),
            pltpu.VMEM((S, bins, width), BF16),
            pltpu.VMEM((q_rows, width), BF16),
            pltpu.VMEM((mixed_rows, width), BF16),
            pltpu.VMEM((6 * bins, mixed_rows), BF16),
            pltpu.VMEM((variants, S * owner_rows, 2 * bins), F32),
            pltpu.VMEM((Z, 2 * bins, width), BF16),
            pltpu.VMEM((2 * bins, tracks), F32),
            pltpu.VMEM((S, owner_rows, tracks), F32),
            pltpu.VMEM((S, owner_rows, tracks), F32),
            dma((6,)),
            dma((S, PARTS)),
            dma((S, PARTS)),
            dma((2,)),
            dma((2,)),
            dma((Z, CHUNKS)),
            dma((Z, CHUNKS)),
            dma((Z, CHUNKS)),
            dma((S,)),
            dma((S,)),
        ],
        compiler_params=pltpu.CompilerParams(
            collective_id=0, has_side_effects=True, vmem_limit_bytes=56 * 1024 * 1024
        ),
    )(
        seq_input[0],
        skip_input[0],
        norm_gain,
        conv_weight,
        head_bias[None],
        exon_start,
        exon_length,
        exon_gene,
        gene_order,
        query_weight,
        key_weight,
        value_weight,
        head_weight,
    )


def solution(mesh):
    placed = (
        P(("grp", "pair"), "seq", None),
        P(("grp", "pair"), "seq", None),
        P(),
        P(),
        P(),
        P(),
        P(),
        P(None, "pair"),
        P("pair"),
        P("grp", None),
        P("grp", None),
        P("grp", None),
        P("grp", None),
    )
    return jax.shard_map(
        functools.partial(body, mesh.shape["seq"], mesh.shape["pair"]),
        mesh=mesh,
        in_specs=placed,
        out_specs=P("grp", "seq", "pair"),
        check_vma=False,
    )
```
